32 devices in a mesh: groups: 2 (over x), tensor: 8 (over z, y), rep: 2 (over core).
Axes of the slice: x: 2, y: 2, z: 4, core: 2. Of those that a mesh axis runs over, the one named last changes fastest.
Arguments:
- acts: bfloat16 [3, 256, 8192], P(None, ('groups', 'rep'), 'tensor'), parts along dimension 1, may hold values from -6 to 6
- base_projection_weight: bfloat16 [8192, 8192], P(None, 'tensor'), may hold values from -0.0625 to 0.0625
- adapter_down_factors: bfloat16 [32, 8192, 64], P('tensor'), may hold values from -0.0625 to 0.0625
- adapter_up_factors: bfloat16 [32, 64, 8192], P('tensor'), may hold values from -0.75 to 0.75
- requested_adapter_ids: int32 [3, 256], P(None, ('groups', 'rep')), parts along dimension 1, may hold values from 0 to 31, as said below
- slot_of_adapter: int32 [64], P('groups'), parts along dimension 0, may hold values from 0 to 31, as said below
- active_row_counts: int32 [6], P('groups'), parts along dimension 0, may hold values from 32 to 64
Outputs:
- projected: bfloat16 [3, 256, 8192], P(None, ('groups', 'rep'), 'tensor'), parts along dimension 1
The draws below stay inside these ranges and needn't reach their ends.
There are 2 independent parts, one for each index of `groups`. The reference program is written for one: setup_inputs(seed, part) draws one part's arguments, and reference() takes and returns one part's arrays. A program takes and returns all parts, laid end to end along the dimension named above; an argument that names none is the same for every part. Nothing has to cross between parts.
Inputs may be any that keep to these rules, and one draw needn't show every extreme that they name: `requested_adapter_ids`: for each step and each batch shard of 64 rows (rows r * 64 to (r + 1) * 64 - 1), the owner slot_of_adapter[id] // 4 of the rows' ids is the same for at most 16 rows, live or not, and for exactly 16 rows for some owner. `slot_of_adapter`: each slot number appears once.
All inputs are finite; a program needn't handle non-finite values.
Results may differ from the reference program's by a relative error of at most 0.0049.
Values may be sent and summed in bfloat16 or wider, within the bound.
A program may use at most 128 MiB of HBM per device.

```python
import jax
import jax.numpy as jnp
from jax import lax

MODEL_WIDTH = 8192
ADAPTER_RANK = 64
STEPS = 3
ADAPT_DEV = 4
ADAPTER_SLOTS = 32
ROWS_CORE = 64
ROWS = 128
CAP = 16
N_TENSOR = 8
N_REP = 2


def shared_slots(key):
    return jax.random.permutation(jax.random.fold_in(key, 11), ADAPTER_SLOTS).astype(jnp.int32)


def draw_slot_of_adapter(key, part):
    return shared_slots(key)


def draw_requested_adapter_ids(key, part):
    slot_table = shared_slots(key)
    key = jax.random.fold_in(key, 3)
    holder = jnp.argsort(slot_table).astype(jnp.int32)
    keys = jax.random.split(key, STEPS * N_REP)

    def one_block(block_key):
        key_hot, key_rest, key_order, key_local = jax.random.split(block_key, 4)
        hot = jax.random.randint(key_hot, (), 0, N_TENSOR)
        others = (hot + 1 + jnp.arange((N_TENSOR - 1) * CAP) // CAP) % N_TENSOR
        others = jax.random.permutation(key_rest, others)
        owners = jnp.concatenate([jnp.full((CAP,), hot, jnp.int32), others[:ROWS_CORE - CAP].astype(jnp.int32)])
        owners = jax.random.permutation(key_order, owners)
        local = jax.random.randint(key_local, (ROWS_CORE,), 0, ADAPT_DEV)
        return holder[owners * ADAPT_DEV + local]
    ids = jax.vmap(one_block)(keys)
    return ids.reshape(STEPS, N_REP * ROWS_CORE).astype(jnp.int32)


def block_levels(key, extent, shards, least, top_value):
    def one(dim, shards_of):
        draws = jax.random.uniform(jax.random.fold_in(jax.random.fold_in(key, 6), dim), (shards_of,), jnp.float32, least / len(shards), top_value / len(shards))
        return jnp.repeat(jnp.exp(draws), extent[dim] // shards_of).reshape((-1,) + (1,) * (len(extent) - dim - 1))

    gain = one(*shards[0])
    for cut in shards[1:]:
        gain = gain * one(*cut)
    return gain


def gaussian(key, dims, width, reach, pieces=(), dtype=jnp.bfloat16):
    drawn = jax.random.normal(key, dims, jnp.float32) * width
    if len(pieces) > 0:
        drawn = block_levels(key, dims, pieces, -0.22, 0.18) * drawn
    return jnp.clip(drawn, min=-reach, max=reach).astype(dtype)


def setup_inputs(seed: int = 0, part: int = 0) -> dict:
    seeds = jax.random.split(jax.random.key(seed), 8)
    part_keys = jax.random.split(jax.random.fold_in(seeds[7], part), 8)
    return {
        "acts": gaussian(part_keys[0], (STEPS, ROWS, MODEL_WIDTH), 1.0, 6.0, ((1, 2), (2, 8))),
        "base_projection_weight": gaussian(seeds[1], (MODEL_WIDTH, MODEL_WIDTH), MODEL_WIDTH ** -0.5, 0.0625, ((1, 8),)),
        "adapter_down_factors": gaussian(seeds[2], (ADAPTER_SLOTS, MODEL_WIDTH, ADAPTER_RANK), MODEL_WIDTH ** -0.5, 0.0625, ((0, 8),)),
        "adapter_up_factors": gaussian(seeds[3], (ADAPTER_SLOTS, ADAPTER_RANK, MODEL_WIDTH), ADAPTER_RANK ** -0.5, 0.75, ((0, 8),)),
        "requested_adapter_ids": draw_requested_adapter_ids(jax.random.fold_in(jax.random.fold_in(seeds[7], part), 71), part),
        "slot_of_adapter": draw_slot_of_adapter(jax.random.fold_in(jax.random.fold_in(seeds[7], part), 71), part),
        "active_row_counts": jax.random.randint(part_keys[6], (STEPS,), ROWS_CORE // 2, ROWS_CORE + 1).astype(jnp.int32),
    }


def reference(acts, base_projection_weight, adapter_down_factors, adapter_up_factors, requested_adapter_ids, slot_of_adapter, active_row_counts):
    block = 16
    results = []
    for step in range(STEPS):
        rows_now = acts[step]
        base = jnp.dot(rows_now, base_projection_weight, preferred_element_type=jnp.float32)
        slots = slot_of_adapter[requested_adapter_ids[step]].astype(jnp.int32)
        alive = (jnp.arange(ROWS) % ROWS_CORE) < active_row_counts[step]

        def one_block(pair):
            rows_blk, slot_block_table = pair
            down_factor = adapter_down_factors[slot_block_table].astype(jnp.float32)
            low = jnp.einsum('bd,bdr->br', rows_blk.astype(jnp.float32), down_factor).astype(jnp.bfloat16)
            up_factor = adapter_up_factors[slot_block_table].astype(jnp.float32)
            return jnp.einsum('br,brd->bd', low.astype(jnp.float32), up_factor).astype(jnp.bfloat16)

        delta = lax.map(one_block, (rows_now.reshape(ROWS // block, block, MODEL_WIDTH), slots.reshape(ROWS // block, block)))
        delta = delta.reshape(ROWS, MODEL_WIDTH).astype(jnp.float32)
        delta = jnp.where(alive[:, None], delta, jnp.float32(0.0))
        results.append((base + delta).astype(jnp.bfloat16))
    return jnp.stack(results, axis=0)
```

```python
import functools

import jax
import jax.numpy as jnp
from jax import lax
from jax.experimental import pallas as pl
from jax.experimental.pallas import tpu as pltpu
from jax.sharding import PartitionSpec as P

CAP = 16
VMEM_LIMIT = 60 * 1024 * 1024


def grid_of(n):
    short = 1
    while (short * 2) * (short * 2) <= n:
        short *= 2
    return n // short, short


def position_of(index, n):
    long, short = grid_of(n)
    a, b = index // short, index % short
    inner = (b + short - 1) // short
    odd = a % 2
    snake = a * (short - 1) + (1 - odd) * (b - 1) + odd * (short - 1 - b)
    return inner * snake + (1 - inner) * (n - 1 - a)


def index_of(position, n):
    long, short = grid_of(n)
    back = position // (long * (short - 1))
    a = position // (short - 1)
    c = position % (short - 1)
    odd = a % 2
    b = 1 + (1 - odd) * c + odd * (short - 2 - c)
    return (1 - back) * (a * short + b) + back * ((n - 1 - position) * short)


def kernel(
    n,
    acts_ref,
    ids_ref,
    table_ref,
    counts_ref,
    w_hbm,
    down_hbm,
    up_hbm,
    out_ref,
    w_v,
    down_v,
    up_v,
    g,
    acc,
    low,
    scatter,
    d_send,
    d_recv,
    w_sem,
    down_sem,
    up_sem,
    g_send_sem,
    g_recv_sem,
    a_send_sem,
    a_recv_sem,
):
    steps, rows, width = acts_ref.shape
    holds, rank, _ = down_hbm.shape
    half = rows // 2
    hops = n // 2
    me = lax.axis_index("tensor")
    place = position_of(me, n)
    ring = (
        index_of((place + 1) % n, n),
        index_of((place + n - 1) % n, n),
    )

    def slot_of(direction, hop):
        return min(1 + direction + 2 * hop, n - 1)

    def origin(slot):
        hop = (slot + 1) // 2
        away = n - hop if slot % 2 == 1 else hop
        return index_of((place + away) % n, n)

    def w_copies(slot):
        at = pl.ds(pl.multiple_of(origin(slot) * width, width), width)
        return (
            pltpu.make_async_copy(w_hbm.at[at], w_v.at[slot], w_sem.at[slot]),
            pltpu.make_async_copy(
                down_hbm.at[:, :, at], down_v.at[slot], down_sem.at[slot]
            ),
        )

    up_copy = pltpu.make_async_copy(up_hbm, up_v, up_sem)

    for slot in range(n):
        for copy in w_copies(slot):
            copy.start()
    up_copy.start()

    barrier = pltpu.get_barrier_semaphore()

    def greet(offset, carry):
        pl.semaphore_signal(
            barrier,
            inc=1,
            device_id={"tensor": (me + offset) % n},
            device_id_type=pl.DeviceIdType.MESH,
        )
        return carry

    lax.fori_loop(1, n, greet, 0)
    pl.semaphore_wait(barrier, n - 1)

    def hop_copy(direction, s, hop, part):
        at = pl.ds(part * half, half)
        if hop == 0:
            src = acts_ref.at[s, at]
        else:
            src = g.at[s, slot_of(direction, hop - 1), at]
        return pltpu.make_async_remote_copy(
            src_ref=src,
            dst_ref=g.at[s, slot_of(direction, hop), at],
            send_sem=g_send_sem.at[s, direction, hop, part],
            recv_sem=g_recv_sem.at[s, direction, hop, part],
            device_id={"tensor": ring[direction]},
            device_id_type=pl.DeviceIdType.MESH,
        )

    def travels(direction, hop, part):
        return hop < hops - 1 or (hop == hops - 1 and part == direction)

    def start_first(s):
        for part in range(2):
            for direction in range(2):
                if travels(direction, 0, part):
                    hop_copy(direction, s, 0, part).start()

    def term_copy(s, offset):
        return pltpu.make_async_remote_copy(
            src_ref=d_send.at[s, offset],
            dst_ref=d_recv.at[s, pl.ds(pl.multiple_of(me * CAP, CAP), CAP)],
            send_sem=a_send_sem.at[s, offset],
            recv_sem=a_recv_sem.at[s, offset],
            device_id={"tensor": (me + offset) % n},
            device_id_type=pl.DeviceIdType.MESH,
        )

    def take_weights(s, slot):
        @pl.when(s == 0)
        def _():
            for copy in w_copies(slot):
                copy.wait()

    def add_product(s, slot, block):
        base = jnp.dot(block, w_v[slot], preferred_element_type=jnp.float32)
        small = lax.dot_general(
            block,
            down_v[slot].reshape(holds * rank, width),
            (((1,), (1,)), ((), ())),
            preferred_element_type=jnp.float32,
        )
        if slot == 0:
            acc[s] = base
            low[...] = small
        else:
            acc[s] += base
            low[...] += small

    f32 = jnp.float32

    def iota(shape, dim):
        return lax.broadcasted_iota(jnp.int32, shape, dim).astype(f32)

    def finish(s):
        def arrived(offset, carry):
            term_copy(s, offset).wait_recv()
            return carry

        lax.fori_loop(1, n, arrived, 0)
        delta = jnp.dot(scatter[s], d_recv[s], preferred_element_type=f32)
        out_ref[s] = (acc[s] + delta).astype(out_ref.dtype)

    start_first(0)

    def one_step(s, carry):
        take_weights(s, 0)
        add_product(s, 0, acts_ref[s])

        ids_row = ids_ref[pl.ds(s, 1), :].astype(f32)
        table = table_ref[...].astype(f32)
        down_at, across = iota((rows, rows), 0), iota((rows, rows), 1)
        eye = down_at == across
        ids_col = jnp.sum(jnp.where(eye, ids_row, 0.0), axis=1, keepdims=True)
        found = ids_col == iota((rows, table.shape[1]), 1)
        slot_col = jnp.sum(jnp.where(found, table, 0.0), axis=1, keepdims=True)
        owner_col = jnp.floor((slot_col + 0.5) * (1.0 / holds))
        local_col = slot_col - owner_col * holds
        owner_row = jnp.sum(jnp.where(eye, owner_col, 0.0), axis=0, keepdims=True)
        same = owner_col == owner_row
        rank_col = jnp.sum(
            jnp.where(same & (across < down_at), 1.0, 0.0), axis=1, keepdims=True
        )
        rank_row = jnp.sum(
            jnp.where(same & (down_at < across), 1.0, 0.0), axis=0, keepdims=True
        )
        alive = iota((rows, 1), 0) < counts_ref[s].astype(f32)
        target = jnp.where(alive, owner_col * CAP + rank_col, -1.0)
        scatter[s] = jnp.where(
            target == iota((rows, n * CAP), 1), 1.0, 0.0
        ).astype(jnp.bfloat16)
        pick = jnp.where(
            (rank_row == iota((CAP, rows), 0)) & (owner_row == me.astype(f32)), 1.0, 0.0
        ).astype(jnp.bfloat16)

        for hop in range(hops):
            if hop == max(hops - 2, 0):

                @pl.when(s + 1 < steps)
                def _():
                    start_first(s + 1)

            for part in range(2):
                for direction in range(2):
                    if travels(direction, hop, part):
                        hop_copy(direction, s, hop, part).wait_recv()
                        if travels(direction, hop + 1, part):
                            hop_copy(direction, s, hop + 1, part).start()
            for slot in sorted({slot_of(0, hop), slot_of(1, hop)}):
                take_weights(s, slot)
                add_product(s, slot, g[s, slot])

        held = lax.broadcasted_iota(jnp.int32, (rows, holds * rank), 1) // rank
        masked = jnp.where(local_col == held.astype(f32), low[...], 0.0)
        packed = jnp.dot(
            pick, masked.astype(jnp.bfloat16), preferred_element_type=f32
        ).astype(jnp.bfloat16)

        @pl.when(s == 0)
        def _():
            up_copy.wait()

        def term(device):
            at = pl.ds(pl.multiple_of(device * width, width), width)
            factor = up_v[:, :, at].reshape(holds * rank, width)
            return jnp.dot(packed, factor, preferred_element_type=f32).astype(
                jnp.bfloat16
            )

        def send_term(offset, carry):
            d_send[s, offset] = term((me + offset) % n)
            term_copy(s, offset).start()
            return carry

        lax.fori_loop(1, n, send_term, 0)
        d_recv[s, pl.ds(pl.multiple_of(me * CAP, CAP), CAP)] = term(me)

        @pl.when(s > 0)
        def _():
            finish(s - 1)

        return carry

    lax.fori_loop(0, steps, one_step, 0)
    finish(steps - 1)

    def drain(s, carry):
        for hop in range(hops):
            for part in range(2):
                for direction in range(2):
                    if travels(direction, hop, part):
                        hop_copy(direction, s, hop, part).wait_send()

        def sent(offset, inner):
            term_copy(s, offset).wait_send()
            return inner

        return lax.fori_loop(1, n, sent, carry)

    lax.fori_loop(0, steps, drain, 0)


def per_device(
    acts,
    base_projection_weight,
    adapter_down_factors,
    adapter_up_factors,
    requested_adapter_ids,
    slot_of_adapter,
    active_row_counts,
):
    n = lax.axis_size("tensor")
    steps, rows, width = acts.shape
    holds, full, rank = adapter_down_factors.shape
    bf16 = jnp.bfloat16
    hops = n // 2
    vmem = pl.BlockSpec(memory_space=pltpu.VMEM)
    anywhere = pl.BlockSpec(memory_space=pl.ANY)
    return pl.pallas_call(
        functools.partial(kernel, n),
        out_shape=jax.ShapeDtypeStruct(acts.shape, bf16),
        in_specs=[
            vmem,
            vmem,
            vmem,
            pl.BlockSpec(memory_space=pltpu.SMEM),
            anywhere,
            anywhere,
            anywhere,
        ],
        out_specs=vmem,
        scratch_shapes=[
            pltpu.VMEM((n, width, width), bf16),
            pltpu.VMEM((n, holds, rank, width), bf16),
            pltpu.VMEM((holds, rank, full), bf16),
            pltpu.VMEM((steps, n, rows, width), bf16),
            pltpu.VMEM((steps, rows, width), jnp.float32),
            pltpu.VMEM((rows, holds * rank), jnp.float32),
            pltpu.VMEM((steps, rows, n * CAP), bf16),
            pltpu.VMEM((steps, n, CAP, width), bf16),
            pltpu.VMEM((steps, n * CAP, width), bf16),
            pltpu.SemaphoreType.DMA((n,)),
            pltpu.SemaphoreType.DMA((n,)),
            pltpu.SemaphoreType.DMA,
            pltpu.SemaphoreType.DMA((steps, 2, hops, 2)),
            pltpu.SemaphoreType.DMA((steps, 2, hops, 2)),
            pltpu.SemaphoreType.DMA((steps, n)),
            pltpu.SemaphoreType.DMA((steps, n)),
        ],
        compiler_params=pltpu.CompilerParams(
            collective_id=0, has_side_effects=True, vmem_limit_bytes=VMEM_LIMIT
        ),
        cost_estimate=pl.CostEstimate(
            flops=2 * steps * rows * full * (width + holds * rank),
            bytes_accessed=2 * full * (width + 2 * holds * rank),
            transcendentals=0,
        ),
    )(
        acts,
        requested_adapter_ids,
        slot_of_adapter.reshape(1, -1),
        active_row_counts,
        base_projection_weight,
        jnp.swapaxes(adapter_down_factors, 1, 2),
        adapter_up_factors,
    )


def solution(mesh):
    placed = (
        P(None, ("groups", "rep"), "tensor"),
        P(None, "tensor"),
        P("tensor", None, None),
        P("tensor", None, None),
        P(None, ("groups", "rep")),
        P("groups"),
        P("groups"),
    )
    return jax.shard_map(
        per_device,
        mesh=mesh,
        in_specs=placed,
        out_specs=P(None, ("groups", "rep"), "tensor"),
        check_vma=False,
    )
```

```python
import functools

import jax
import jax.numpy as jnp
from jax import lax
from jax.experimental import pallas as pl
from jax.experimental.pallas import tpu as pltpu
from jax.sharding import PartitionSpec as P

CAP = 16
VMEM_LIMIT = 60 * 1024 * 1024


def grid_of(n):
    short = 1
    while (short * 2) * (short * 2) <= n:
        short *= 2
    return n // short, short


def position_of(index, n):
    long, short = grid_of(n)
    a, b = index // short, index % short
    inner = (b + short - 1) // short
    odd = a % 2
    snake = a * (short - 1) + (1 - odd) * (b - 1) + odd * (short - 1 - b)
    return inner * snake + (1 - inner) * (n - 1 - a)


def index_of(position, n):
    long, short = grid_of(n)
    back = position // (long * (short - 1))
    a = position // (short - 1)
    c = position % (short - 1)
    odd = a % 2
    b = 1 + (1 - odd) * c + odd * (short - 2 - c)
    return (1 - back) * (a * short + b) + back * ((n - 1 - position) * short)


def kernel(
    n,
    acts_ref,
    ids_ref,
    table_ref,
    counts_ref,
    w_hbm,
    down_hbm,
    up_hbm,
    out_ref,
    acts_v,
    w_v,
    down_v,
    up_v,
    g,
    acc,
    low,
    scatter,
    pick,
    keep,
    d_send,
    d_recv,
    own_sem,
    w_sem,
    down_sem,
    up_sem,
    g_send_sem,
    g_recv_sem,
    a_send_sem,
    a_recv_sem,
):
    steps, rows, width = acts_ref.shape
    holds, rank, _ = down_hbm.shape
    half = rows // 2
    hops = n // 2
    me = lax.axis_index("tensor")
    place = position_of(me, n)
    ring = (
        index_of((place + 1) % n, n),
        index_of((place + n - 1) % n, n),
    )

    def slot_of(direction, hop):
        return min(1 + direction + 2 * hop, n - 1)

    def origin(slot):
        hop = (slot + 1) // 2
        away = n - hop if slot % 2 == 1 else hop
        return index_of((place + away) % n, n)

    def w_copies(slot):
        at = pl.ds(pl.multiple_of(origin(slot) * width, width), width)
        return (
            pltpu.make_async_copy(w_hbm.at[at], w_v.at[slot], w_sem.at[slot]),
            pltpu.make_async_copy(
                down_hbm.at[:, :, at], down_v.at[slot], down_sem.at[slot]
            ),
        )

    up_copy = pltpu.make_async_copy(up_hbm, up_v, up_sem)

    own_copy = pltpu.make_async_copy(acts_ref, acts_v, own_sem)
    own_copy.start()
    barrier = pltpu.get_barrier_semaphore()

    def greet(offset, carry):
        pl.semaphore_signal(
            barrier,
            inc=1,
            device_id={"tensor": (me + offset) % n},
            device_id_type=pl.DeviceIdType.MESH,
        )
        return carry

    lax.fori_loop(1, n, greet, 0)
    for copy in w_copies(0):
        copy.start()
    pl.semaphore_wait(barrier, n - 1)

    def hop_copy(direction, s, hop, part):
        at = pl.ds(part * half, half)
        if hop == 0:
            src = acts_ref.at[s, at]
        else:
            src = g.at[slot_of(direction, hop - 1), s, at]
        return pltpu.make_async_remote_copy(
            src_ref=src,
            dst_ref=g.at[slot_of(direction, hop), s, at],
            send_sem=g_send_sem.at[s, direction, hop, part],
            recv_sem=g_recv_sem.at[s, direction, hop, part],
            device_id={"tensor": ring[direction]},
            device_id_type=pl.DeviceIdType.MESH,
        )

    def travels(direction, hop, part):
        return hop < hops - 1 or (hop == hops - 1 and part == direction)

    def term_copy(s, offset):
        return pltpu.make_async_remote_copy(
            src_ref=d_send.at[s, offset],
            dst_ref=d_recv.at[s, pl.ds(pl.multiple_of(me * CAP, CAP), CAP)],
            send_sem=a_send_sem.at[s, offset],
            recv_sem=a_recv_sem.at[s, offset],
            device_id={"tensor": (me + offset) % n},
            device_id_type=pl.DeviceIdType.MESH,
        )

    def add_low(slot, s, block):
        at = pl.ds(s * rows, block.shape[0])
        small = lax.dot_general(
            block,
            down_v[slot].reshape(holds * rank, width),
            (((1,), (1,)), ((), ())),
            preferred_element_type=jnp.float32,
        )
        low[at] = small if slot == 0 else low[at] + small

    def add_base(slot, block):
        base = jnp.dot(block, w_v[slot], preferred_element_type=jnp.float32)
        acc[...] = base if slot == 0 else acc[...] + base

    f32 = jnp.float32

    def iota(shape, dim):
        return lax.broadcasted_iota(jnp.int32, shape, dim).astype(f32)

    pieces = [
        (s, part, direction)
        for s in range(steps)
        for part in range(2)
        for direction in range(2)
    ]
    for s, part, direction in pieces:
        if travels(direction, 0, part):
            hop_copy(direction, s, 0, part).start()
    for slot in range(1, n):
        for copy in w_copies(slot):
            copy.start()
    up_copy.start()

    def place_rows(s, carry):
        ids_row = ids_ref[pl.ds(s, 1), :].astype(f32)
        table = table_ref[...].astype(f32)
        down_at, across = iota((rows, rows), 0), iota((rows, rows), 1)
        eye = down_at == across
        ids_col = jnp.sum(jnp.where(eye, ids_row, 0.0), axis=1, keepdims=True)
        found = ids_col == iota((rows, table.shape[1]), 1)
        slot_col = jnp.sum(jnp.where(found, table, 0.0), axis=1, keepdims=True)
        owner_col = jnp.floor((slot_col + 0.5) * (1.0 / holds))
        local_col = slot_col - owner_col * holds
        owner_row = jnp.sum(jnp.where(eye, owner_col, 0.0), axis=0, keepdims=True)
        same = owner_col == owner_row
        rank_col = jnp.sum(
            jnp.where(same & (across < down_at), 1.0, 0.0), axis=1, keepdims=True
        )
        rank_row = jnp.sum(
            jnp.where(same & (down_at < across), 1.0, 0.0), axis=0, keepdims=True
        )
        alive = iota((rows, 1), 0) < counts_ref[s].astype(f32)
        target = jnp.where(alive, owner_col * CAP + rank_col, -1.0)
        scatter[s] = jnp.where(
            target == iota((rows, n * CAP), 1), 1.0, 0.0
        ).astype(jnp.bfloat16)
        pick[s] = jnp.where(
            (rank_row == iota((CAP, rows), 0)) & (owner_row == me.astype(f32)), 1.0, 0.0
        ).astype(jnp.bfloat16)
        held = lax.broadcasted_iota(jnp.int32, (rows, holds * rank), 1) // rank
        keep[s] = jnp.where(local_col == held.astype(f32), 1.0, 0.0)
        return carry

    def await_weights(slot):
        for copy in w_copies(slot):
            copy.wait()

    own_copy.wait()
    await_weights(0)
    own = acts_v[...].reshape(steps * rows, width)
    add_base(0, own)
    add_low(0, 0, own)
    lax.fori_loop(0, steps, place_rows, 0)

    def forward(hop, s, part, direction):
        if travels(direction, hop, part):
            hop_copy(direction, s, hop, part).wait_recv()
            if travels(direction, hop + 1, part):
                hop_copy(direction, s, hop + 1, part).start()

    for hop in range(hops - 1):
        for s, part, direction in pieces:
            forward(hop, s, part, direction)
        for slot in (slot_of(0, hop), slot_of(1, hop)):
            await_weights(slot)
            block = g[slot].reshape(steps * rows, width)
            add_base(slot, block)
            add_low(slot, 0, block)
    await_weights(n - 1)
    up_copy.wait()

    for s in range(steps):
        for part in range(2):
            for direction in range(2):
                forward(hops - 1, s, part, direction)
        add_low(n - 1, s, g[n - 1, s])
        masked = jnp.where(keep[s] > 0.5, low[pl.ds(s * rows, rows)], 0.0)
        packed = jnp.dot(
            pick[s], masked.astype(jnp.bfloat16), preferred_element_type=f32
        ).astype(jnp.bfloat16)

        def term(device, packed=packed):
            at = pl.ds(pl.multiple_of(device * width, width), width)
            factor = up_v[:, :, at].reshape(holds * rank, width)
            return jnp.dot(packed, factor, preferred_element_type=f32).astype(
                jnp.bfloat16
            )

        def send_term(offset, carry, s=s, term=term):
            d_send[s, offset] = term((me + offset) % n)
            term_copy(s, offset).start()
            return carry

        lax.fori_loop(1, n, send_term, 0)
        d_recv[s, pl.ds(pl.multiple_of(me * CAP, CAP), CAP)] = term(me)

    add_base(n - 1, g[n - 1].reshape(steps * rows, width))

    def finish(s, carry):
        def arrived(offset, inner):
            term_copy(s, offset).wait_recv()
            return inner

        lax.fori_loop(1, n, arrived, 0)
        delta = jnp.dot(scatter[s], d_recv[s], preferred_element_type=f32)
        base = acc[pl.ds(pl.multiple_of(s * rows, rows), rows)]
        out_ref[s] = (base + delta).astype(out_ref.dtype)
        return carry

    lax.fori_loop(0, steps, finish, 0)

    def drain(s, carry):
        for hop in range(hops):
            for part in range(2):
                for direction in range(2):
                    if travels(direction, hop, part):
                        hop_copy(direction, s, hop, part).wait_send()

        def sent(offset, inner):
            term_copy(s, offset).wait_send()
            return inner

        return lax.fori_loop(1, n, sent, carry)

    lax.fori_loop(0, steps, drain, 0)


def per_device(
    acts,
    base_projection_weight,
    adapter_down_factors,
    adapter_up_factors,
    requested_adapter_ids,
    slot_of_adapter,
    active_row_counts,
):
    n = lax.axis_size("tensor")
    steps, rows, width = acts.shape
    holds, full, rank = adapter_down_factors.shape
    bf16 = jnp.bfloat16
    hops = n // 2
    vmem = pl.BlockSpec(memory_space=pltpu.VMEM)
    anywhere = pl.BlockSpec(memory_space=pl.ANY)
    return pl.pallas_call(
        functools.partial(kernel, n),
        out_shape=jax.ShapeDtypeStruct(acts.shape, bf16),
        in_specs=[
            anywhere,
            vmem,
            vmem,
            pl.BlockSpec(memory_space=pltpu.SMEM),
            anywhere,
            anywhere,
            anywhere,
        ],
        out_specs=vmem,
        scratch_shapes=[
            pltpu.VMEM((steps, rows, width), bf16),
            pltpu.VMEM((n, width, width), bf16),
            pltpu.VMEM((n, holds, rank, width), bf16),
            pltpu.VMEM((holds, rank, full), bf16),
            pltpu.VMEM((n, steps, rows, width), bf16),
            pltpu.VMEM((steps * rows, width), jnp.float32),
            pltpu.VMEM((steps * rows, holds * rank), jnp.float32),
            pltpu.VMEM((steps, rows, n * CAP), bf16),
            pltpu.VMEM((steps, CAP, rows), bf16),
            pltpu.VMEM((steps, rows, holds * rank), jnp.float32),
            pltpu.VMEM((steps, n, CAP, width), bf16),
            pltpu.VMEM((steps, n * CAP, width), bf16),
            pltpu.SemaphoreType.DMA,
            pltpu.SemaphoreType.DMA((n,)),
            pltpu.SemaphoreType.DMA((n,)),
            pltpu.SemaphoreType.DMA,
            pltpu.SemaphoreType.DMA((steps, 2, hops, 2)),
            pltpu.SemaphoreType.DMA((steps, 2, hops, 2)),
            pltpu.SemaphoreType.DMA((steps, n)),
            pltpu.SemaphoreType.DMA((steps, n)),
        ],
        compiler_params=pltpu.CompilerParams(
            collective_id=0, has_side_effects=True, vmem_limit_bytes=VMEM_LIMIT
        ),
        cost_estimate=pl.CostEstimate(
            flops=2 * steps * rows * full * (width + holds * rank),
            bytes_accessed=2 * full * (width + 2 * holds * rank),
            transcendentals=0,
        ),
    )(
        acts,
        requested_adapter_ids,
        slot_of_adapter.reshape(1, -1),
        active_row_counts,
        base_projection_weight,
        jnp.swapaxes(adapter_down_factors, 1, 2),
        adapter_up_factors,
    )


def solution(mesh):
    placed = (
        P(None, ("groups", "rep"), "tensor"),
        P(None, "tensor"),
        P("tensor", None, None),
        P("tensor", None, None),
        P(None, ("groups", "rep")),
        P("groups"),
        P("groups"),
    )
    return jax.shard_map(
        per_device,
        mesh=mesh,
        in_specs=placed,
        out_specs=P(None, ("groups", "rep"), "tensor"),
        check_vma=False,
    )
```
